32 devices in a mesh: groups: 2 (over y), hosts: 8 (over z, x), tensor: 2 (over core).
Axes of the slice: x: 2, y: 2, z: 4, core: 2. Of those that a mesh axis runs over, the one named last changes fastest.
Arguments:
- context_queries: bfloat16 [2048, 8192], P(('groups', 'hosts'), 'tensor'), parts along dimension 0, may hold values from -6 to 6
- context_keys: bfloat16 [2048, 1024], P(('groups', 'hosts'), 'tensor'), parts along dimension 0, may hold values from -6 to 6
- context_values: bfloat16 [2048, 1024], P(('groups', 'hosts'), 'tensor'), parts along dimension 0, may hold values from -6 to 6
- doc_ids: int32 [2048], P(('groups', 'hosts')), parts along dimension 0, may hold values from 0 to 31, never falling along the last dimension, each value on 1 to 128 neighbouring positions
- query_token_rows: bfloat16 [16, 8192], P(('groups', 'hosts'), 'tensor'), parts along dimension 0, may hold values from -6 to 6
- span_start: int32 [16], P(('groups', 'hosts')), parts along dimension 0, may hold values from 0 to 511
Outputs:
- block_out: bfloat16 [2048, 8192], P(('groups', 'hosts'), 'tensor'), parts along dimension 0
- answer: bfloat16 [16, 8192], P(('groups', 'hosts'), 'tensor'), parts along dimension 0
The draws below stay inside these ranges and needn't reach their ends.
There are 2 independent parts, one for each index of `groups`. The reference program is written for one: setup_inputs(seed, part) draws one part's arguments, and reference() takes and returns one part's arrays. A program takes and returns all parts, laid end to end along the dimension named above; each array names one. Nothing has to cross between parts.
All inputs are finite; a program needn't handle non-finite values.
Results may differ from the reference program's by a relative error of at most 0.0043.
Values may be sent and summed in bfloat16 or wider, within the bound.
A program may use at most 64 MiB of HBM per device.

```python
import math
import jax
import jax.numpy as jnp
import numpy as np
from jax import lax

QUERY_HEADS = 64
KEY_VALUE_HEADS = 8
HEAD_SIZE = 128
BLOCK_TOKENS = 128
CONTEXT_TOKENS = 1024
QUERY_COUNT = 8
N_HOSTS = 8


def coarse_rows(key, count_rows, heads):
    return jnp.clip(jax.random.normal(jax.random.fold_in(key, 5), (count_rows, heads, HEAD_SIZE), jnp.float32), -6.0, 6.0)


def draw_context_keys(key, part):
    base_offset = coarse_rows(jax.random.fold_in(key, 11), CONTEXT_TOKENS, KEY_VALUE_HEADS)
    return base_offset.reshape(CONTEXT_TOKENS, KEY_VALUE_HEADS * HEAD_SIZE).astype(jnp.bfloat16)


def draw_context_queries(key, part):
    base_offset = coarse_rows(jax.random.fold_in(key, 13), CONTEXT_TOKENS, QUERY_HEADS)
    return base_offset.reshape(CONTEXT_TOKENS, QUERY_HEADS * HEAD_SIZE).astype(jnp.bfloat16)


def draw_query_token_rows(key, part):
    base_offset = coarse_rows(jax.random.fold_in(key, 17), QUERY_COUNT, QUERY_HEADS)
    return base_offset.reshape(QUERY_COUNT, QUERY_HEADS * HEAD_SIZE).astype(jnp.bfloat16)


def touch_ends(drawn, stream_key, low, high):
    extent = drawn.shape
    spot = [jax.random.randint(jax.random.fold_in(stream_key, axis), (), 0, extent[axis]) for axis in range(len(extent))]
    drawn = drawn.at[tuple(spot)].set(low)
    longest = extent.index(max(extent))
    spot[longest] = (spot[longest] + 1) % extent[longest]
    return drawn.at[tuple(spot)].set(high)


def levels(key, dims, shards, low, high):
    gain = 1.0
    for axis_at, shards_of in shards:
        heights = jax.random.uniform(jax.random.fold_in(jax.random.fold_in(key, 6), axis_at), (shards_of,), jnp.float32, low / len(shards), high / len(shards))
        gain = gain * jnp.repeat(jnp.exp(heights), dims[axis_at] // shards_of).reshape((-1,) + (1,) * (len(dims) - 1 - axis_at))
    return gain


def split_up(count, total, most, lean):
    weights = [(1 << 20) // math.isqrt(grade ** lean) + 1 for grade in range(2, count + 1)]
    rest, holding = total - most - (count - 1), [1] * (count - 1)
    while rest > 0:
        movable = [i for i in range(count - 1) if holding[i] < most]
        pool, left = sum([weights[i] for i in movable]), rest
        for i in movable:
            extra = min(most - holding[i], max(1, left * weights[i] // pool), rest)
            holding[i] = holding[i] + extra
            rest = rest - extra
    return np.array([most] + holding)


def ragged_sizes(rng, number_of, total, bound, lean):
    if number_of == 2:
        one = jax.random.randint(rng, (), max(1, total - bound), min(bound, total - 1) + 1)
        return jnp.stack([one, total - one])
    sizes = jnp.asarray(split_up(number_of, total, bound, lean), jnp.int32)
    couples = (number_of - 1) // 2
    giver, taker = sizes[1:1 + 2 * couples:2], sizes[2:2 + 2 * couples:2]
    room = jnp.minimum(giver - 1, bound - taker)
    shifted = jax.random.randint(jax.random.fold_in(rng, 1), (couples,), 0, 1 << 20) % (room + 1)
    sizes = sizes.at[1:1 + 2 * couples:2].set(giver - shifted).at[2:2 + 2 * couples:2].set(taker + shifted)
    return sizes[jax.random.permutation(jax.random.fold_in(rng, 2), number_of)]


def scatter_about(key, dims, scale, reach, cuts=(), kind=jnp.bfloat16):
    loudness = levels(key, dims, cuts, -0.22, 0.18) if cuts else 1.0
    drawn = jax.random.normal(key, dims, jnp.float32) * scale * loudness
    return jnp.minimum(jnp.maximum(drawn, -reach), reach).astype(kind)


def setup_inputs(seed: int = 0, part: int = 0) -> dict:
    arg_keys = jax.random.split(jax.random.key(seed), 7)
    part_splits = jax.random.split(jax.random.fold_in(arg_keys[6], part), 7)
    return {
        "context_queries": draw_context_queries(jax.random.fold_in(jax.random.fold_in(arg_keys[6], part), 71), part),
        "context_keys": draw_context_keys(jax.random.fold_in(jax.random.fold_in(arg_keys[6], part), 71), part),
        "context_values": scatter_about(part_splits[2], (CONTEXT_TOKENS, KEY_VALUE_HEADS * HEAD_SIZE), 1.0, 6.0, ((0, 8), (1, 2))),
        "doc_ids": jnp.searchsorted(jnp.cumsum(ragged_sizes(part_splits[3], 4 * N_HOSTS, CONTEXT_TOKENS, BLOCK_TOKENS, 2)), jnp.arange(CONTEXT_TOKENS), side="right").astype(jnp.int32),
        "query_token_rows": draw_query_token_rows(jax.random.fold_in(jax.random.fold_in(arg_keys[6], part), 71), part),
        "span_start": touch_ends(jax.random.randint(part_splits[5], (QUERY_COUNT,), 0, CONTEXT_TOKENS // 2), jax.random.fold_in(part_splits[5], 1), 0, (CONTEXT_TOKENS // 2) - 1).astype(jnp.int32),
    }


MASKED_SCORE = -1e30


def reference(context_queries, context_keys, context_values, doc_ids, query_token_rows, span_start):
    factor = float(HEAD_SIZE) ** -0.5
    heads_per_group = QUERY_HEADS // KEY_VALUE_HEADS
    queries_of_block = context_queries.reshape(N_HOSTS, BLOCK_TOKENS, KEY_VALUE_HEADS, heads_per_group, HEAD_SIZE)
    keys_of_block = context_keys.reshape(N_HOSTS, BLOCK_TOKENS, KEY_VALUE_HEADS, HEAD_SIZE)
    values_of_block = context_values.reshape(N_HOSTS, BLOCK_TOKENS, KEY_VALUE_HEADS, HEAD_SIZE)
    block_docs = doc_ids.reshape(N_HOSTS, BLOCK_TOKENS)
    anchor_keys = keys_of_block[0]
    anchor_values = values_of_block[0]
    positions = jnp.arange(BLOCK_TOKENS, dtype=jnp.int32)
    causal = positions[None, :] <= positions[:, None]

    def block_pass(operands):
        block_index, query_part, key_part, value_part, doc_part = operands
        key_rows = jnp.concatenate([anchor_keys, key_part], 0).astype(jnp.float32)
        value_rows = jnp.concatenate([anchor_values, value_part], 0).astype(jnp.float32)
        own_visible = causal & (doc_part[:, None] == doc_part[None, :])
        front_visible = jnp.broadcast_to(block_index > 0, (BLOCK_TOKENS, BLOCK_TOKENS))
        visible = jnp.concatenate([front_visible, own_visible], 1)[:, None, None, :]
        scores = jnp.einsum('rkgd,skd->rkgs', query_part.astype(jnp.float32), key_rows) * factor
        peak_score = jnp.max(jnp.where(visible, scores, MASKED_SCORE), -1, keepdims=True)
        weights = jnp.where(visible, jnp.exp(scores - peak_score), 0.0)
        totals = jnp.sum(weights, -1)
        rounded = lax.optimization_barrier(weights.astype(jnp.bfloat16)).astype(jnp.float32)
        output = jnp.einsum('rkgs,skd->rkgd', rounded, value_rows) / totals[..., None]
        return output.astype(jnp.bfloat16).reshape(BLOCK_TOKENS, QUERY_HEADS * HEAD_SIZE)

    block_out = lax.map(block_pass, (jnp.arange(N_HOSTS, dtype=jnp.int32), queries_of_block, keys_of_block, values_of_block, block_docs))
    block_out = block_out.reshape(CONTEXT_TOKENS, QUERY_HEADS * HEAD_SIZE)

    query_single = query_token_rows.reshape(QUERY_COUNT, KEY_VALUE_HEADS, heads_per_group, HEAD_SIZE).astype(jnp.float32)

    def query_pass(running, operands):
        block_index, key_part, value_part = operands
        old_peak, old_total, old_acc = running
        scores = jnp.einsum('qkgd,skd->qkgs', query_single, key_part.astype(jnp.float32)) * factor
        key_positions = block_index * BLOCK_TOKENS + positions
        visible = (key_positions[None, :] >= span_start[:, None])[:, None, None, :]
        peak_score = jnp.max(jnp.where(visible, scores, MASKED_SCORE), -1)
        weights = jnp.where(visible, jnp.exp(scores - peak_score[..., None]), 0.0)
        totals = jnp.sum(weights, -1)
        rounded = lax.optimization_barrier(weights.astype(jnp.bfloat16)).astype(jnp.float32)
        partial_acc = jnp.einsum('qkgs,skd->qkgd', rounded, value_part.astype(jnp.float32))
        fresh = jnp.maximum(old_peak, peak_score)
        old_scale = jnp.exp(old_peak - fresh)
        new_scale = jnp.exp(peak_score - fresh)
        return (fresh, old_total * old_scale + totals * new_scale,
                old_acc * old_scale[..., None] + partial_acc * new_scale[..., None]), None

    start_offset = (jnp.full((QUERY_COUNT, KEY_VALUE_HEADS, heads_per_group), MASKED_SCORE, jnp.float32),
             jnp.zeros((QUERY_COUNT, KEY_VALUE_HEADS, heads_per_group), jnp.float32),
             jnp.zeros((QUERY_COUNT, KEY_VALUE_HEADS, heads_per_group, HEAD_SIZE), jnp.float32))
    final, unused = lax.scan(query_pass, start_offset, (jnp.arange(N_HOSTS, dtype=jnp.int32), keys_of_block, values_of_block))
    answer = (final[2] / final[1][..., None]).astype(jnp.bfloat16).reshape(QUERY_COUNT, QUERY_HEADS * HEAD_SIZE)
    return block_out, answer
```

```python
import functools
import math

import jax
import jax.numpy as jnp
from jax import lax
from jax.experimental import pallas as pl
from jax.experimental.pallas import tpu as pltpu
from jax.sharding import PartitionSpec as P

HEAD_SIZE = 128
MASKED_SCORE = -1e30
SPAN_BASE = 128
MESH = pl.DeviceIdType.MESH


def each(n, body):
    if n <= 16:
        for k in range(1, n):
            body(k)
    else:
        pl.loop(1, n)(body)


def kernel(
    n, kv, group, block,
    q_hbm, k_hbm, v_hbm, docs_ref, rows_ref, span_ref,
    out_hbm, answer_ref,
    qbuf, obuf, own, anchor, bias, qrow, qall, psend, precv,
    in_sem, anc_sem, out_sem, qs_sem, qr_sem, ps_sem, pr_sem, down_sem, side_sem, ar_sem,
):
    me = lax.axis_index("hosts")
    row, col = me // 2, me % 2
    rows = n // 2
    half = kv // 2
    heads = kv * group
    width = group * HEAD_SIZE
    factor = float(HEAD_SIZE) ** -0.5 * math.log2(math.e)
    is_root = me == 0

    def load_kv(c, buf, sem):
        cols = slice(c * HEAD_SIZE, (c + 1) * HEAD_SIZE)
        return (
            pltpu.make_async_copy(k_hbm.at[:, cols], buf.at[c, 0], sem.at[c, 0]),
            pltpu.make_async_copy(v_hbm.at[:, cols], buf.at[c, 1], sem.at[c, 1]),
        )

    def load_q(c):
        return pltpu.make_async_copy(
            q_hbm.at[:, c * width:(c + 1) * width], qbuf.at[c], in_sem.at[c, 2]
        )

    @pl.when(is_root)
    def _():
        for c in range(kv):
            for copy in load_kv(c, anchor, anc_sem):
                copy.start()

    for c in range(kv):
        for copy in load_kv(c, own, in_sem):
            copy.start()
    for c in range(kv):
        load_q(c).start()

    barrier = pltpu.get_barrier_semaphore()

    def greet(k):
        pl.semaphore_signal(
            barrier, inc=1, device_id={"hosts": lax.rem(me + k, n)}, device_id_type=MESH
        )

    each(n, greet)

    for h in range(heads):
        qrow[pl.ds(h, 1), :] = rows_ref[:, h * HEAD_SIZE:(h + 1) * HEAD_SIZE].astype(jnp.float32)
    span = span_ref[0]
    qrow[heads:heads + 8, :] = jnp.full((8, HEAD_SIZE), span // SPAN_BASE, jnp.int32).astype(jnp.float32)
    qrow[heads + 8:heads + 16, :] = jnp.full((8, HEAD_SIZE), span % SPAN_BASE, jnp.int32).astype(jnp.float32)
    qall[me] = qrow[...].astype(jnp.bfloat16)

    pl.semaphore_wait(barrier, n - 1)

    def send_down(c):
        return pltpu.make_async_remote_copy(
            anchor.at[c], anchor.at[c], down_sem.at[c], ar_sem.at[c],
            device_id={"hosts": me + 2}, device_id_type=MESH,
        )

    def send_side(c):
        return pltpu.make_async_remote_copy(
            anchor.at[c], anchor.at[c], side_sem.at[c], ar_sem.at[c],
            device_id={"hosts": me + 1 - 2 * col}, device_id_type=MESH,
        )

    def arrived(c):
        pltpu.make_async_copy(anchor.at[c], anchor.at[c], ar_sem.at[c]).wait()

    @pl.when(is_root)
    def _():
        for c in range(kv):
            for copy in load_kv(c, anchor, anc_sem):
                copy.wait()
        for c in range(half):
            if rows > 1:
                send_down(c).start()
            send_side(half + c).start()
        for c in range(half):
            send_side(c).start()

    def q_copy(k):
        return pltpu.make_async_remote_copy(
            qall.at[me], qall.at[me], qs_sem.at[k], qr_sem.at[me],
            device_id={"hosts": lax.rem(me + k, n)}, device_id_type=MESH,
        )

    each(n, lambda k: q_copy(k).start())

    docs = jnp.broadcast_to(docs_ref[...].astype(jnp.float32), (block, block))
    at_row = lax.broadcasted_iota(jnp.int32, (block, block), 0)
    at_col = lax.broadcasted_iota(jnp.int32, (block, block), 1)
    shown = (at_col <= at_row) & (docs == docs.T)
    bias[...] = jnp.where(shown, 0.0, MASKED_SCORE)

    for c in range(kv):
        for copy in load_kv(c, own, in_sem):
            copy.wait()

    def from_host(k):
        return lax.rem(me + n - k, n)

    def q_arrived(k):
        source = from_host(k)
        pltpu.make_async_copy(qall.at[source], qall.at[source], qr_sem.at[source]).wait()

    each(n, q_arrived)

    def p_copy(k):
        to = lax.rem(me + k, n)
        return pltpu.make_async_remote_copy(
            psend.at[to], precv.at[me], ps_sem.at[k], pr_sem.at[me],
            device_id={"hosts": to}, device_id_type=MESH,
        )

    tokens = qall[...].astype(jnp.float32)
    spans = tokens[:, heads:heads + 8] * SPAN_BASE + tokens[:, heads + 8:heads + 16]
    place = lax.broadcasted_iota(jnp.int32, (n, 8, block), 2) + me * block
    seen = (place.astype(jnp.float32) >= spans).reshape(n * group, block)
    lane = lax.broadcasted_iota(jnp.int32, (n, group, HEAD_SIZE), 2) // 16
    stats = jnp.zeros((n, group, HEAD_SIZE), jnp.float32)
    ones = jnp.ones((block, HEAD_SIZE), jnp.bfloat16)
    for c in range(kv):
        part = tokens[:, c * group:(c + 1) * group].reshape(n * group, HEAD_SIZE)
        scores = lax.dot_general(
            part.astype(jnp.bfloat16), own[c, 0], (((1,), (1,)), ((), ())),
            preferred_element_type=jnp.float32,
        )
        scores = jnp.where(seen, scores, MASKED_SCORE)
        peak = jnp.max(scores, -1, keepdims=True)
        weights = jnp.where(seen, jnp.exp2((scores - peak) * factor), 0.0)
        acc = jnp.dot(
            weights.astype(jnp.bfloat16), jnp.concatenate([own[c, 1], ones], 1),
            preferred_element_type=jnp.float32,
        )
        psend[:, c * group:(c + 1) * group, :] = acc[:, :HEAD_SIZE].reshape(n, group, HEAD_SIZE)
        total = acc[:, HEAD_SIZE:].reshape(n, group, HEAD_SIZE)
        stats = jnp.where(lane == 2 * c, total, stats)
        peak = jnp.broadcast_to(peak, (n * group, HEAD_SIZE)).reshape(n, group, HEAD_SIZE)
        stats = jnp.where(lane == 2 * c + 1, peak, stats)
    psend[:, heads:heads + group, :] = stats
    each(n, lambda k: p_copy(k).start())
    precv[me] = psend[me]

    for j in range(half):
        c = col * half + j

        @pl.when(me > 0)
        def _():
            arrived(c)

            @pl.when(row < rows - 1)
            def _():
                send_down(c).start()

            @pl.when(row > 0)
            def _():
                send_side(c).start()

    def put(c):
        return pltpu.make_async_copy(
            obuf.at[c],
            out_hbm.at[:, pl.ds(pl.multiple_of(c * width, width), width)],
            out_sem.at[c],
        )

    for c in range(kv):
        load_q(c).wait()
    own_bias = jnp.concatenate([bias[...], bias[...]], 0)
    wide_ones = jnp.ones((2 * block, HEAD_SIZE), jnp.bfloat16)

    @pl.loop(0, kv)
    def _(j):
        c = lax.rem(col * half + j, kv)

        @pl.when((me > 0) & (j >= half))
        def _():
            arrived(c)

        keys = jnp.concatenate([anchor[c, 0], own[c, 0]], 0)
        values = jnp.concatenate([anchor[c, 1], own[c, 1]], 0)
        values = jnp.concatenate([values, wide_ones], 1)
        for g in range(0, group, 2):
            queries = jnp.concatenate(
                [qbuf[c, :, (g + i) * HEAD_SIZE:(g + i + 1) * HEAD_SIZE] for i in range(2)], 0
            )
            scores = lax.dot_general(
                queries, keys, (((1,), (1,)), ((), ())), preferred_element_type=jnp.float32
            )
            front = jnp.where(is_root, MASKED_SCORE, scores[:, :block])
            back = scores[:, block:] + own_bias
            top = jnp.max(jnp.maximum(front, back), -1, keepdims=True)
            weights = jnp.concatenate(
                [jnp.exp2((front - top) * factor), jnp.exp2((back - top) * factor)], 1
            ).astype(jnp.bfloat16)
            acc = jnp.dot(weights, values, preferred_element_type=jnp.float32)
            result = (acc[:, :HEAD_SIZE] / acc[:, HEAD_SIZE:]).astype(jnp.bfloat16)
            for i in range(2):
                obuf[c, :, (g + i) * HEAD_SIZE:(g + i + 1) * HEAD_SIZE] = result[i * block:(i + 1) * block]
        put(c).start()

    def p_arrived(k):
        source = from_host(k)
        pltpu.make_async_copy(precv.at[source], precv.at[source], pr_sem.at[source]).wait()

    each(n, p_arrived)
    stats = precv[:, heads:heads + group, :]
    for c in range(kv):
        total = stats[:, :, 32 * c:32 * c + 1]
        peak = stats[:, :, 32 * c + 16:32 * c + 17]
        scale = jnp.exp2((peak - jnp.max(peak, 0, keepdims=True)) * factor)
        total = jnp.sum(scale * total, 0)
        merged = jnp.sum(scale * precv[:, c * group:(c + 1) * group, :], 0)
        answer_ref[c * group:(c + 1) * group, :] = merged / total

    each(n, lambda k: q_copy(k).wait_send())
    each(n, lambda k: p_copy(k).wait_send())

    @pl.when(is_root)
    def _():
        for c in range(half):
            if rows > 1:
                send_down(c).wait_send()
            send_side(half + c).wait_send()
        for c in range(half):
            send_side(c).wait_send()

    for j in range(half):
        c = col * half + j

        @pl.when((me > 0) & (row < rows - 1))
        def _():
            send_down(c).wait_send()

        @pl.when(row > 0)
        def _():
            send_side(c).wait_send()

    for c in range(kv):
        put(c).wait()


def on_device(n, context_queries, context_keys, context_values, doc_ids, query_token_rows, span_start):
    block = context_queries.shape[0]
    kv = context_keys.shape[1] // HEAD_SIZE
    group = context_queries.shape[1] // context_keys.shape[1]
    heads = kv * group
    width = group * HEAD_SIZE
    any_spec = pl.BlockSpec(memory_space=pl.ANY)
    vmem_spec = pl.BlockSpec(memory_space=pltpu.VMEM)
    dma = pltpu.SemaphoreType.DMA
    block_out, answer = pl.pallas_call(
        functools.partial(kernel, n, kv, group, block),
        out_shape=(
            jax.ShapeDtypeStruct(context_queries.shape, jnp.bfloat16),
            jax.ShapeDtypeStruct((heads, HEAD_SIZE), jnp.float32),
        ),
        in_specs=[any_spec, any_spec, any_spec, vmem_spec, vmem_spec, pl.BlockSpec(memory_space=pltpu.SMEM)],
        out_specs=(any_spec, vmem_spec),
        scratch_shapes=[
            pltpu.VMEM((kv, block, width), jnp.bfloat16),
            pltpu.VMEM((kv, block, width), jnp.bfloat16),
            pltpu.VMEM((kv, 2, block, HEAD_SIZE), jnp.bfloat16),
            pltpu.VMEM((kv, 2, block, HEAD_SIZE), jnp.bfloat16),
            pltpu.VMEM((block, block), jnp.float32),
            pltpu.VMEM((heads + 16, HEAD_SIZE), jnp.float32),
            pltpu.VMEM((n, heads + 16, HEAD_SIZE), jnp.bfloat16),
            pltpu.VMEM((n, heads + 8, HEAD_SIZE), jnp.float32),
            pltpu.VMEM((n, heads + 8, HEAD_SIZE), jnp.float32),
            dma((kv, 3)), dma((kv, 2)), dma((kv,)),
            dma((n,)), dma((n,)), dma((n,)), dma((n,)),
            dma((kv,)), dma((kv,)), dma((kv,)),
        ],
        compiler_params=pltpu.CompilerParams(
            collective_id=0, has_side_effects=True, vmem_limit_bytes=40 * 1024 * 1024
        ),
    )(
        context_queries, context_keys, context_values,
        doc_ids.reshape(1, block), query_token_rows, span_start,
    )
    return block_out, answer.reshape(1, heads * HEAD_SIZE).astype(jnp.bfloat16)


def solution(mesh):
    in_specs = (
        P(("groups", "hosts"), "tensor"),
        P(("groups", "hosts"), "tensor"),
        P(("groups", "hosts"), "tensor"),
        P(("groups", "hosts")),
        P(("groups", "hosts"), "tensor"),
        P(("groups", "hosts")),
    )
    out_specs = (P(("groups", "hosts"), "tensor"), P(("groups", "hosts"), "tensor"))
    return jax.shard_map(
        functools.partial(on_device, mesh.shape["hosts"]),
        mesh=mesh, in_specs=in_specs, out_specs=out_specs, check_vma=False,
    )
```

```python
import functools
import math

import jax
import jax.numpy as jnp
from jax import lax
from jax.experimental import pallas as pl
from jax.experimental.pallas import tpu as pltpu
from jax.sharding import PartitionSpec as P

HEAD_SIZE = 128
MASKED_SCORE = -1e30
SPAN_BASE = 128
MESH = pl.DeviceIdType.MESH


def each(n, body):
    if n <= 16:
        for k in range(1, n):
            body(k)
    else:
        pl.loop(1, n)(body)


def kernel(
    n, kv, group, block,
    q_hbm, k_hbm, v_hbm, docs_hbm, rows_hbm, span_ref,
    out_hbm, answer_ref,
    docs_ref, rows_ref, qbuf, obuf, own, anchor, bias, qrow, qall, psend, precv,
    in_sem, anc_sem, out_sem, small_sem, qs_sem, qr_sem, ps_sem, pr_sem, scatter_sem, pass_sem, ar_sem,
):
    me = lax.axis_index("hosts")
    pieces = 2 * kv
    spread = n // pieces
    mine = me // spread
    heads = kv * group
    width = group * HEAD_SIZE
    factor = float(HEAD_SIZE) ** -0.5 * math.log2(math.e)
    is_root = me == 0

    def load_kv(c, buf, sem):
        cols = slice(c * HEAD_SIZE, (c + 1) * HEAD_SIZE)
        return (
            pltpu.make_async_copy(k_hbm.at[:, cols], buf.at[c, 0], sem.at[c, 0]),
            pltpu.make_async_copy(v_hbm.at[:, cols], buf.at[c, 1], sem.at[c, 1]),
        )

    def load_q(c):
        return pltpu.make_async_copy(
            q_hbm.at[:, c * width:(c + 1) * width], qbuf.at[c], in_sem.at[c, 2]
        )

    small = (
        pltpu.make_async_copy(rows_hbm, rows_ref, small_sem.at[0]),
        pltpu.make_async_copy(docs_hbm, docs_ref, small_sem.at[1]),
    )
    for copy in small:
        copy.start()

    @pl.when(is_root)
    def _():
        for c in range(kv):
            for copy in load_kv(c, anchor, anc_sem):
                copy.start()

    for c in range(kv):
        for copy in load_kv(c, own, in_sem):
            copy.start()
    for c in range(kv):
        load_q(c).start()

    barrier = pltpu.get_barrier_semaphore()

    def greet(k):
        pl.semaphore_signal(
            barrier, inc=1, device_id={"hosts": lax.rem(me + k, n)}, device_id_type=MESH
        )

    each(n, greet)

    for copy in small:
        copy.wait()

    for h in range(heads):
        qrow[pl.ds(h, 1), :] = rows_ref[:, h * HEAD_SIZE:(h + 1) * HEAD_SIZE].astype(jnp.float32)
    span = span_ref[0]
    qrow[heads:heads + 8, :] = jnp.full((8, HEAD_SIZE), span // SPAN_BASE, jnp.int32).astype(jnp.float32)
    qrow[heads + 8:heads + 16, :] = jnp.full((8, HEAD_SIZE), span % SPAN_BASE, jnp.int32).astype(jnp.float32)
    qall[me] = qrow[...].astype(jnp.bfloat16)

    pl.semaphore_wait(barrier, n - 1)

    def scatter(p):
        piece = anchor.at[p // 2, p % 2]
        return pltpu.make_async_remote_copy(
            piece, piece, scatter_sem.at[p], ar_sem.at[p],
            device_id={"hosts": jnp.int32(p * spread)}, device_id_type=MESH,
        )

    def pass_on(k):
        piece = anchor.at[mine // 2, mine % 2]
        return pltpu.make_async_remote_copy(
            piece, piece, pass_sem.at[k], ar_sem.at[mine],
            device_id={"hosts": lax.rem(me + k, n)}, device_id_type=MESH,
        )

    def arrived(p):
        piece = anchor.at[p // 2, p % 2]
        pltpu.make_async_copy(piece, piece, ar_sem.at[p]).wait()

    def when_not_root(k, act):
        @pl.when(lax.rem(me + k, n) > 0)
        def _():
            act(pass_on(k))

    @pl.when(is_root)
    def _():
        for c in range(kv):
            for copy in load_kv(c, anchor, anc_sem):
                copy.wait()
        for p in reversed(range(1, pieces)):
            scatter(p).start()
        each(n, lambda k: pass_on(k).start())

    def q_copy(k):
        return pltpu.make_async_remote_copy(
            qall.at[me], qall.at[me], qs_sem.at[k], qr_sem.at[me],
            device_id={"hosts": lax.rem(me + k, n)}, device_id_type=MESH,
        )

    each(n, lambda k: q_copy(k).start())

    is_owner = (lax.rem(me, spread) == 0) & (me > 0)

    @pl.when(is_owner)
    def _():
        arrived(mine)
        each(n, lambda k: when_not_root(k, lambda copy: copy.start()))

    docs = jnp.broadcast_to(docs_ref[...].astype(jnp.float32), (block, block))
    at_row = lax.broadcasted_iota(jnp.int32, (block, block), 0)
    at_col = lax.broadcasted_iota(jnp.int32, (block, block), 1)
    shown = (at_col <= at_row) & (docs == docs.T)
    bias[...] = jnp.where(shown, 0.0, MASKED_SCORE)

    for c in range(kv):
        for copy in load_kv(c, own, in_sem):
            copy.wait()

    def from_host(k):
        return lax.rem(me + n - k, n)

    def q_arrived(k):
        source = from_host(k)
        pltpu.make_async_copy(qall.at[source], qall.at[source], qr_sem.at[source]).wait()

    each(n, q_arrived)

    def p_copy(k):
        to = lax.rem(me + k, n)
        return pltpu.make_async_remote_copy(
            psend.at[to], precv.at[me], ps_sem.at[k], pr_sem.at[me],
            device_id={"hosts": to}, device_id_type=MESH,
        )

    tokens = qall[...].astype(jnp.float32)
    spans = tokens[:, heads:heads + 8] * SPAN_BASE + tokens[:, heads + 8:heads + 16]
    place = lax.broadcasted_iota(jnp.int32, (n, 8, block), 2) + me * block
    seen = (place.astype(jnp.float32) >= spans).reshape(n * group, block)
    lane = lax.broadcasted_iota(jnp.int32, (n, group, HEAD_SIZE), 2) // 16
    stats = jnp.zeros((n, group, HEAD_SIZE), jnp.float32)
    ones = jnp.ones((block, HEAD_SIZE), jnp.bfloat16)
    for c in range(kv):
        part = tokens[:, c * group:(c + 1) * group].reshape(n * group, HEAD_SIZE)
        scores = lax.dot_general(
            part.astype(jnp.bfloat16), own[c, 0], (((1,), (1,)), ((), ())),
            preferred_element_type=jnp.float32,
        )
        scores = jnp.where(seen, scores, MASKED_SCORE)
        peak = jnp.max(scores, -1, keepdims=True)
        weights = jnp.where(seen, jnp.exp2((scores - peak) * factor), 0.0)
        acc = jnp.dot(
            weights.astype(jnp.bfloat16), jnp.concatenate([own[c, 1], ones], 1),
            preferred_element_type=jnp.float32,
        )
        psend[:, c * group:(c + 1) * group, :] = acc[:, :HEAD_SIZE].reshape(n, group, HEAD_SIZE)
        total = acc[:, HEAD_SIZE:].reshape(n, group, HEAD_SIZE)
        stats = jnp.where(lane == 2 * c, total, stats)
        peak = jnp.broadcast_to(peak, (n * group, HEAD_SIZE)).reshape(n, group, HEAD_SIZE)
        stats = jnp.where(lane == 2 * c + 1, peak, stats)
    psend[:, heads:heads + group, :] = stats
    each(n, lambda k: p_copy(k).start())
    precv[me] = psend[me]

    def put(c):
        return pltpu.make_async_copy(
            obuf.at[c],
            out_hbm.at[:, pl.ds(pl.multiple_of(c * width, width), width)],
            out_sem.at[c],
        )

    for c in range(kv):
        load_q(c).wait()
    own_bias = jnp.concatenate([bias[...], bias[...]], 0)
    wide_ones = jnp.ones((2 * block, HEAD_SIZE), jnp.bfloat16)

    @pl.loop(0, kv)
    def _(j):
        c = lax.rem(mine // 2 + j, kv)
        for i in range(2):

            @pl.when((me > 0) & ~(is_owner & (2 * c + i == mine)))
            def _():
                arrived(2 * c + i)

        keys = jnp.concatenate([anchor[c, 0], own[c, 0]], 0)
        values = jnp.concatenate([anchor[c, 1], own[c, 1]], 0)
        values = jnp.concatenate([values, wide_ones], 1)
        for g in range(0, group, 2):
            queries = jnp.concatenate(
                [qbuf[c, :, (g + i) * HEAD_SIZE:(g + i + 1) * HEAD_SIZE] for i in range(2)], 0
            )
            scores = lax.dot_general(
                queries, keys, (((1,), (1,)), ((), ())), preferred_element_type=jnp.float32
            )
            front = jnp.where(is_root, MASKED_SCORE, scores[:, :block])
            back = scores[:, block:] + own_bias
            top = jnp.max(jnp.maximum(front, back), -1, keepdims=True)
            weights = jnp.concatenate(
                [jnp.exp2((front - top) * factor), jnp.exp2((back - top) * factor)], 1
            ).astype(jnp.bfloat16)
            acc = jnp.dot(weights, values, preferred_element_type=jnp.float32)
            result = (acc[:, :HEAD_SIZE] / acc[:, HEAD_SIZE:]).astype(jnp.bfloat16)
            for i in range(2):
                obuf[c, :, (g + i) * HEAD_SIZE:(g + i + 1) * HEAD_SIZE] = result[i * block:(i + 1) * block]
        put(c).start()

    def p_arrived(k):
        source = from_host(k)
        pltpu.make_async_copy(precv.at[source], precv.at[source], pr_sem.at[source]).wait()

    each(n, p_arrived)
    stats = precv[:, heads:heads + group, :]
    for c in range(kv):
        total = stats[:, :, 32 * c:32 * c + 1]
        peak = stats[:, :, 32 * c + 16:32 * c + 17]
        scale = jnp.exp2((peak - jnp.max(peak, 0, keepdims=True)) * factor)
        total = jnp.sum(scale * total, 0)
        merged = jnp.sum(scale * precv[:, c * group:(c + 1) * group, :], 0)
        answer_ref[c * group:(c + 1) * group, :] = merged / total

    each(n, lambda k: q_copy(k).wait_send())
    each(n, lambda k: p_copy(k).wait_send())

    @pl.when(is_root)
    def _():
        for p in range(1, pieces):
            scatter(p).wait_send()
        each(n, lambda k: pass_on(k).wait_send())

    @pl.when(is_owner)
    def _():
        each(n, lambda k: when_not_root(k, lambda copy: copy.wait_send()))

    for c in range(kv):
        put(c).wait()


def on_device(n, context_queries, context_keys, context_values, doc_ids, query_token_rows, span_start):
    block = context_queries.shape[0]
    kv = context_keys.shape[1] // HEAD_SIZE
    group = context_queries.shape[1] // context_keys.shape[1]
    heads = kv * group
    width = group * HEAD_SIZE
    any_spec = pl.BlockSpec(memory_space=pl.ANY)
    hbm_spec = pl.BlockSpec(memory_space=pltpu.HBM)
    vmem_spec = pl.BlockSpec(memory_space=pltpu.VMEM)
    dma = pltpu.SemaphoreType.DMA
    block_out, answer = pl.pallas_call(
        functools.partial(kernel, n, kv, group, block),
        out_shape=(
            jax.ShapeDtypeStruct(context_queries.shape, jnp.bfloat16),
            jax.ShapeDtypeStruct((heads, HEAD_SIZE), jnp.float32),
        ),
        in_specs=[hbm_spec] * 5 + [pl.BlockSpec(memory_space=pltpu.SMEM)],
        out_specs=(any_spec, vmem_spec),
        scratch_shapes=[
            pltpu.VMEM((1, block), jnp.int32),
            pltpu.VMEM(query_token_rows.shape, jnp.bfloat16),
            pltpu.VMEM((kv, block, width), jnp.bfloat16),
            pltpu.VMEM((kv, block, width), jnp.bfloat16),
            pltpu.VMEM((kv, 2, block, HEAD_SIZE), jnp.bfloat16),
            pltpu.VMEM((kv, 2, block, HEAD_SIZE), jnp.bfloat16),
            pltpu.VMEM((block, block), jnp.float32),
            pltpu.VMEM((heads + 16, HEAD_SIZE), jnp.float32),
            pltpu.VMEM((n, heads + 16, HEAD_SIZE), jnp.bfloat16),
            pltpu.VMEM((n, heads + 8, HEAD_SIZE), jnp.float32),
            pltpu.VMEM((n, heads + 8, HEAD_SIZE), jnp.float32),
            dma((kv, 3)), dma((kv, 2)), dma((kv,)), dma((2,)),
            dma((n,)), dma((n,)), dma((n,)), dma((n,)),
            dma((2 * kv,)), dma((n,)), dma((2 * kv,)),
        ],
        compiler_params=pltpu.CompilerParams(
            collective_id=0, has_side_effects=True, vmem_limit_bytes=40 * 1024 * 1024
        ),
    )(
        context_queries, context_keys, context_values,
        doc_ids.reshape(1, block), query_token_rows, span_start,
    )
    return block_out, answer.reshape(1, heads * HEAD_SIZE).astype(jnp.bfloat16)


def solution(mesh):
    in_specs = (
        P(("groups", "hosts"), "tensor"),
        P(("groups", "hosts"), "tensor"),
        P(("groups", "hosts"), "tensor"),
        P(("groups", "hosts")),
        P(("groups", "hosts"), "tensor"),
        P(("groups", "hosts")),
    )
    out_specs = (P(("groups", "hosts"), "tensor"), P(("groups", "hosts"), "tensor"))
    return jax.shard_map(
        functools.partial(on_device, mesh.shape["hosts"]),
        mesh=mesh, in_specs=in_specs, out_specs=out_specs, check_vma=False,
    )
```

```python
import functools
import math

import jax
import jax.numpy as jnp
from jax import lax
from jax.experimental import pallas as pl
from jax.experimental.pallas import tpu as pltpu
from jax.sharding import PartitionSpec as P

HEAD_SIZE = 128
MASKED_SCORE = -1e30
SPAN_BASE = 128
MESH = pl.DeviceIdType.MESH


def each(n, body):
    if n <= 16:
        for k in range(1, n):
            body(k)
    else:
        pl.loop(1, n)(body)


def kernel(
    n, kv, group, block,
    q_hbm, k_hbm, v_hbm, docs_hbm, rows_hbm, span_ref,
    out_hbm, answer_ref,
    docs_ref, rows_ref, qbuf, obuf, own, anchor, bias, qrow, qall, psend, precv,
    in_sem, anc_sem, out_sem, small_sem, qs_sem, qr_sem, ps_sem, pr_sem, scatter_sem, pass_sem, ar_sem,
):
    me = lax.axis_index("hosts")
    pieces = 2 * kv
    spread = n // pieces
    mine = me // spread
    heads = kv * group
    width = group * HEAD_SIZE
    factor = float(HEAD_SIZE) ** -0.5 * math.log2(math.e)
    is_root = me == 0

    def load_kv(c, buf, sem):
        cols = slice(c * HEAD_SIZE, (c + 1) * HEAD_SIZE)
        return (
            pltpu.make_async_copy(k_hbm.at[:, cols], buf.at[c, 0], sem.at[c, 0]),
            pltpu.make_async_copy(v_hbm.at[:, cols], buf.at[c, 1], sem.at[c, 1]),
        )

    def load_q(c):
        return pltpu.make_async_copy(
            q_hbm.at[:, c * width:(c + 1) * width], qbuf.at[c], in_sem.at[c, 2]
        )

    small = (
        pltpu.make_async_copy(rows_hbm, rows_ref, small_sem.at[0]),
        pltpu.make_async_copy(docs_hbm, docs_ref, small_sem.at[1]),
    )
    for copy in small:
        copy.start()

    @pl.when(is_root)
    def _():
        for c in range(kv):
            for copy in load_kv(c, anchor, anc_sem):
                copy.start()

    for c in range(kv):
        for copy in load_kv(c, own, in_sem):
            copy.start()
    for c in range(kv):
        load_q(c).start()

    barrier = pltpu.get_barrier_semaphore()

    def greet(k):
        pl.semaphore_signal(
            barrier, inc=1, device_id={"hosts": lax.rem(me + k, n)}, device_id_type=MESH
        )

    each(n, greet)

    for copy in small:
        copy.wait()

    for h in range(heads):
        qrow[pl.ds(h, 1), :] = rows_ref[:, h * HEAD_SIZE:(h + 1) * HEAD_SIZE].astype(jnp.float32)
    span = span_ref[0]
    qrow[heads:heads + 8, :] = jnp.full((8, HEAD_SIZE), span // SPAN_BASE, jnp.int32).astype(jnp.float32)
    qrow[heads + 8:heads + 16, :] = jnp.full((8, HEAD_SIZE), span % SPAN_BASE, jnp.int32).astype(jnp.float32)
    qall[me] = qrow[...].astype(jnp.bfloat16)

    pl.semaphore_wait(barrier, n - 1)

    def scatter(p):
        piece = anchor.at[p // 2, p % 2]
        return pltpu.make_async_remote_copy(
            piece, piece, scatter_sem.at[p], ar_sem.at[p],
            device_id={"hosts": jnp.int32(p * spread)}, device_id_type=MESH,
        )

    def pass_on(k):
        piece = anchor.at[mine // 2, mine % 2]
        return pltpu.make_async_remote_copy(
            piece, piece, pass_sem.at[k], ar_sem.at[mine],
            device_id={"hosts": lax.rem(me + k, n)}, device_id_type=MESH,
        )

    def arrived(p):
        piece = anchor.at[p // 2, p % 2]
        pltpu.make_async_copy(piece, piece, ar_sem.at[p]).wait()

    def when_not_root(k, act):
        @pl.when(lax.rem(me + k, n) > 0)
        def _():
            act(pass_on(k))

    @pl.when(is_root)
    def _():
        for c in range(kv):
            for copy in load_kv(c, anchor, anc_sem):
                copy.wait()
        for p in reversed(range(1, pieces)):
            scatter(p).start()
        each(n, lambda k: pass_on(k).start())

    def q_copy(k):
        return pltpu.make_async_remote_copy(
            qall.at[me], qall.at[me], qs_sem.at[k], qr_sem.at[me],
            device_id={"hosts": lax.rem(me + k, n)}, device_id_type=MESH,
        )

    each(n, lambda k: q_copy(k).start())

    is_owner = (lax.rem(me, spread) == 0) & (me > 0)

    @pl.when(is_owner)
    def _():
        arrived(mine)
        each(n, lambda k: when_not_root(k, lambda copy: copy.start()))

    docs = jnp.broadcast_to(docs_ref[...].astype(jnp.float32), (block, block))
    at_row = lax.broadcasted_iota(jnp.int32, (block, block), 0)
    at_col = lax.broadcasted_iota(jnp.int32, (block, block), 1)
    shown = (at_col <= at_row) & (docs == docs.T)
    bias[...] = jnp.where(shown, 0.0, MASKED_SCORE)

    for c in range(kv):
        for copy in load_kv(c, own, in_sem):
            copy.wait()

    def from_host(k):
        return lax.rem(me + n - k, n)

    def q_arrived(k):
        source = from_host(k)
        pltpu.make_async_copy(qall.at[source], qall.at[source], qr_sem.at[source]).wait()

    each(n, q_arrived)

    def p_copy(k):
        to = lax.rem(me + k, n)
        return pltpu.make_async_remote_copy(
            psend.at[to], precv.at[me], ps_sem.at[k], pr_sem.at[me],
            device_id={"hosts": to}, device_id_type=MESH,
        )

    tokens = qall[...].astype(jnp.float32)
    spans = tokens[:, heads:heads + 8] * SPAN_BASE + tokens[:, heads + 8:heads + 16]
    place = lax.broadcasted_iota(jnp.int32, (n, 8, block), 2) + me * block
    seen = (place.astype(jnp.float32) >= spans).reshape(n * group, block)
    lane = lax.broadcasted_iota(jnp.int32, (n, group, HEAD_SIZE), 2) // 16
    stats = jnp.zeros((n, group, HEAD_SIZE), jnp.float32)
    ones = jnp.ones((block, HEAD_SIZE), jnp.bfloat16)
    for c in range(kv):
        part = tokens[:, c * group:(c + 1) * group].reshape(n * group, HEAD_SIZE)
        scores = lax.dot_general(
            part.astype(jnp.bfloat16), own[c, 0], (((1,), (1,)), ((), ())),
            preferred_element_type=jnp.float32,
        )
        scores = jnp.where(seen, scores, MASKED_SCORE)
        peak = jnp.max(scores, -1, keepdims=True)
        weights = jnp.where(seen, jnp.exp2((scores - peak) * factor), 0.0)
        acc = jnp.dot(
            weights.astype(jnp.bfloat16), jnp.concatenate([own[c, 1], ones], 1),
            preferred_element_type=jnp.float32,
        )
        psend[:, c * group:(c + 1) * group, :] = acc[:, :HEAD_SIZE].reshape(n, group, HEAD_SIZE)
        total = acc[:, HEAD_SIZE:].reshape(n, group, HEAD_SIZE)
        stats = jnp.where(lane == 2 * c, total, stats)
        peak = jnp.broadcast_to(peak, (n * group, HEAD_SIZE)).reshape(n, group, HEAD_SIZE)
        stats = jnp.where(lane == 2 * c + 1, peak, stats)
    psend[:, heads:heads + group, :] = stats
    each(n, lambda k: p_copy(k).start())
    precv[me] = psend[me]

    def put(c):
        return pltpu.make_async_copy(
            obuf.at[c],
            out_hbm.at[:, pl.ds(pl.multiple_of(c * width, width), width)],
            out_sem.at[c],
        )

    for c in range(kv):
        load_q(c).wait()
    own_bias = jnp.concatenate([bias[...], bias[...]], 0)
    wide_ones = jnp.ones((2 * block, HEAD_SIZE), jnp.bfloat16)

    @pl.loop(0, kv)
    def _(j):
        c = lax.rem(mine // 2 + j, kv)
        for i in range(2):

            @pl.when((me > 0) & ~(is_owner & (2 * c + i == mine)))
            def _():
                arrived(2 * c + i)

        keys = jnp.concatenate([anchor[c, 0], own[c, 0]], 0)
        values = jnp.concatenate([anchor[c, 1], own[c, 1]], 0)
        values = jnp.concatenate([values, wide_ones], 1)
        for g in range(0, group, 2):
            queries = jnp.concatenate(
                [qbuf[c, :, (g + i) * HEAD_SIZE:(g + i + 1) * HEAD_SIZE] for i in range(2)], 0
            )
            scores = lax.dot_general(
                queries, keys, (((1,), (1,)), ((), ())), preferred_element_type=jnp.float32
            )
            front = jnp.where(is_root, MASKED_SCORE, scores[:, :block])
            back = scores[:, block:] + own_bias
            top = jnp.max(jnp.maximum(front, back), -1, keepdims=True)
            weights = jnp.concatenate(
                [jnp.exp2((front - top) * factor), jnp.exp2((back - top) * factor)], 1
            ).astype(jnp.bfloat16)
            acc = jnp.dot(weights, values, preferred_element_type=jnp.float32)
            result = (acc[:, :HEAD_SIZE] / acc[:, HEAD_SIZE:]).astype(jnp.bfloat16)
            for i in range(2):
                obuf[c, :, (g + i) * HEAD_SIZE:(g + i + 1) * HEAD_SIZE] = result[i * block:(i + 1) * block]
        put(c).start()

    def p_arrived(k):
        source = from_host(k)
        pltpu.make_async_copy(precv.at[source], precv.at[source], pr_sem.at[source]).wait()

    each(n, p_arrived)
    stats = precv[:, heads:heads + group, :]
    for c in range(kv):
        total = stats[:, :, 32 * c:32 * c + 1]
        peak = stats[:, :, 32 * c + 16:32 * c + 17]
        scale = jnp.exp2((peak - jnp.max(peak, 0, keepdims=True)) * factor)
        total = jnp.sum(scale * total, 0)
        merged = jnp.sum(scale * precv[:, c * group:(c + 1) * group, :], 0)
        answer_ref[c * group:(c + 1) * group, :] = merged / total

    each(n, lambda k: q_copy(k).wait_send())
    each(n, lambda k: p_copy(k).wait_send())

    @pl.when(is_root)
    def _():
        for p in range(1, pieces):
            scatter(p).wait_send()
        each(n, lambda k: pass_on(k).wait_send())

    @pl.when(is_owner)
    def _():
        each(n, lambda k: when_not_root(k, lambda copy: copy.wait_send()))

    for c in range(kv):
        put(c).wait()


def on_device(n, context_queries, context_keys, context_values, doc_ids, query_token_rows, span_start):
    block = context_queries.shape[0]
    kv = context_keys.shape[1] // HEAD_SIZE
    group = context_queries.shape[1] // context_keys.shape[1]
    heads = kv * group
    width = group * HEAD_SIZE
    any_spec = pl.BlockSpec(memory_space=pl.ANY)
    hbm_spec = pl.BlockSpec(memory_space=pltpu.HBM)
    vmem_spec = pl.BlockSpec(memory_space=pltpu.VMEM)
    dma = pltpu.SemaphoreType.DMA
    block_out, answer = pl.pallas_call(
        functools.partial(kernel, n, kv, group, block),
        out_shape=(
            jax.ShapeDtypeStruct(context_queries.shape, jnp.bfloat16),
            jax.ShapeDtypeStruct((heads, HEAD_SIZE), jnp.float32),
        ),
        in_specs=[hbm_spec] * 5 + [pl.BlockSpec(memory_space=pltpu.SMEM)],
        out_specs=(any_spec, vmem_spec),
        scratch_shapes=[
            pltpu.VMEM((1, block), jnp.int32),
            pltpu.VMEM(query_token_rows.shape, jnp.bfloat16),
            pltpu.VMEM((kv, block, width), jnp.bfloat16),
            pltpu.VMEM((kv, block, width), jnp.bfloat16),
            pltpu.VMEM((kv, 2, block, HEAD_SIZE), jnp.bfloat16),
            pltpu.VMEM((kv, 2, block, HEAD_SIZE), jnp.bfloat16),
            pltpu.VMEM((block, block), jnp.float32),
            pltpu.VMEM((heads + 16, HEAD_SIZE), jnp.float32),
            pltpu.VMEM((n, heads + 16, HEAD_SIZE), jnp.bfloat16),
            pltpu.VMEM((n, heads + 8, HEAD_SIZE), jnp.float32),
            pltpu.VMEM((n, heads + 8, HEAD_SIZE), jnp.float32),
            dma((kv, 3)), dma((kv, 2)), dma((kv,)), dma((2,)),
            dma((n,)), dma((n,)), dma((n,)), dma((n,)),
            dma((2 * kv,)), dma((n,)), dma((2 * kv,)),
        ],
        compiler_params=pltpu.CompilerParams(
            collective_id=0, has_side_effects=True, vmem_limit_bytes=40 * 1024 * 1024
        ),
    )(
        *[
            pltpu.with_memory_space_constraint(array, pltpu.HBM)
            for array in (
                context_queries, context_keys, context_values,
                doc_ids.reshape(1, block), query_token_rows,
            )
        ],
        span_start,
    )
    return block_out, answer.reshape(1, heads * HEAD_SIZE).astype(jnp.bfloat16)


def solution(mesh):
    in_specs = (
        P(("groups", "hosts"), "tensor"),
        P(("groups", "hosts"), "tensor"),
        P(("groups", "hosts"), "tensor"),
        P(("groups", "hosts")),
        P(("groups", "hosts"), "tensor"),
        P(("groups", "hosts")),
    )
    out_specs = (P(("groups", "hosts"), "tensor"), P(("groups", "hosts"), "tensor"))
    return jax.shard_map(
        functools.partial(on_device, mesh.shape["hosts"]),
        mesh=mesh, in_specs=in_specs, out_specs=out_specs, check_vma=False,
    )
```

```python
import functools
import math

import jax
import jax.numpy as jnp
from jax import lax
from jax.experimental import pallas as pl
from jax.experimental.pallas import tpu as pltpu
from jax.sharding import PartitionSpec as P

HEAD_SIZE = 128
MASKED_SCORE = -1e30
SPAN_BASE = 128
MESH = pl.DeviceIdType.MESH


def each(n, body):
    if n <= 16:
        for k in range(1, n):
            body(k)
    else:
        pl.loop(1, n)(body)


def kernel(
    n, kv, group, block,
    q_hbm, k_hbm, v_hbm, docs_hbm, rows_hbm, span_ref,
    out_hbm, answer_ref,
    docs_ref, rows_ref, qbuf, obuf, own, anchor, bias, qrow, qall, pwide, psend, precv,
    in_sem, anc_sem, out_sem, small_sem, qs_sem, qr_sem, ps_sem, pr_sem, scatter_sem, pass_sem, ar_sem,
):
    me = lax.axis_index("hosts")
    length = 2 * kv * block
    owners = min(n - 1, 7)
    size = length // owners // 16 * 16
    extra = length - owners * size
    pieces = [
        (1 + i * ((n - 1) // owners), i * size + (extra if i else 0), size + (0 if i else extra))
        for i in range(owners)
    ]
    heads = kv * group
    width = group * HEAD_SIZE
    factor = float(HEAD_SIZE) ** -0.5 * math.log2(math.e)
    is_root = me == 0

    def load_kv(c, buf, sem):
        cols = slice(c * HEAD_SIZE, (c + 1) * HEAD_SIZE)
        at = 2 * c * block
        return (
            pltpu.make_async_copy(k_hbm.at[:, cols], buf.at[pl.ds(at, block)], sem.at[c, 0]),
            pltpu.make_async_copy(v_hbm.at[:, cols], buf.at[pl.ds(at + block, block)], sem.at[c, 1]),
        )

    def load_q(c):
        return pltpu.make_async_copy(
            q_hbm.at[:, c * width:(c + 1) * width], qbuf.at[c], in_sem.at[c, 2]
        )

    small = (
        pltpu.make_async_copy(rows_hbm, rows_ref, small_sem.at[0]),
        pltpu.make_async_copy(docs_hbm, docs_ref, small_sem.at[1]),
    )
    for copy in small:
        copy.start()

    @pl.when(is_root)
    def _():
        for c in range(kv):
            for copy in load_kv(c, anchor, anc_sem):
                copy.start()

    for c in range(kv):
        for copy in load_kv(c, own, in_sem):
            copy.start()
    for c in range(kv):
        load_q(c).start()

    barrier = pltpu.get_barrier_semaphore()

    def greet(k):
        pl.semaphore_signal(
            barrier, inc=1, device_id={"hosts": lax.rem(me + k, n)}, device_id_type=MESH
        )

    each(n, greet)

    for copy in small:
        copy.wait()

    for h in range(heads):
        qrow[pl.ds(h, 1), :] = rows_ref[:, h * HEAD_SIZE:(h + 1) * HEAD_SIZE].astype(jnp.float32)
    span = span_ref[0]
    qrow[heads:heads + 8, :] = jnp.full((8, HEAD_SIZE), span // SPAN_BASE, jnp.int32).astype(jnp.float32)
    qrow[heads + 8:heads + 16, :] = jnp.full((8, HEAD_SIZE), span % SPAN_BASE, jnp.int32).astype(jnp.float32)
    qall[me] = qrow[...].astype(jnp.bfloat16)

    pl.semaphore_wait(barrier, n - 1)

    def scatter(i):
        host, start, count = pieces[i]
        piece = anchor.at[pl.ds(start, count)]
        return pltpu.make_async_remote_copy(
            piece, piece, scatter_sem.at[i], ar_sem.at[i],
            device_id={"hosts": jnp.int32(host)}, device_id_type=MESH,
        )

    def pass_on(i, k):
        host, start, count = pieces[i]
        piece = anchor.at[pl.ds(start, count)]
        return pltpu.make_async_remote_copy(
            piece, piece, pass_sem.at[k], ar_sem.at[i],
            device_id={"hosts": lax.rem(me + k, n)}, device_id_type=MESH,
        )

    def arrived(i):
        host, start, count = pieces[i]
        piece = anchor.at[pl.ds(start, count)]
        pltpu.make_async_copy(piece, piece, ar_sem.at[i]).wait()

    def when_not_root(i, k, act):
        @pl.when(lax.rem(me + k, n) > 0)
        def _():
            act(pass_on(i, k))

    @pl.when(is_root)
    def _():
        for c in range(kv):
            for copy in load_kv(c, anchor, anc_sem):
                copy.wait()
        for i in reversed(range(owners)):
            scatter(i).start()

    def q_copy(k):
        return pltpu.make_async_remote_copy(
            qall.at[me], qall.at[me], qs_sem.at[k], qr_sem.at[me],
            device_id={"hosts": lax.rem(me + k, n)}, device_id_type=MESH,
        )

    each(n, lambda k: q_copy(k).start())

    for i in range(owners):

        @pl.when(me == pieces[i][0])
        def _():
            arrived(i)
            each(n, lambda k: when_not_root(i, k, lambda copy: copy.start()))

    docs = jnp.broadcast_to(docs_ref[...].astype(jnp.float32), (block, block))
    at_row = lax.broadcasted_iota(jnp.int32, (block, block), 0)
    at_col = lax.broadcasted_iota(jnp.int32, (block, block), 1)
    shown = (at_col <= at_row) & (docs == docs.T)
    bias[...] = jnp.where(shown, 0.0, MASKED_SCORE)

    for c in range(kv):
        for copy in load_kv(c, own, in_sem):
            copy.wait()

    def from_host(k):
        return lax.rem(me + n - k, n)

    def q_arrived(k):
        source = from_host(k)
        pltpu.make_async_copy(qall.at[source], qall.at[source], qr_sem.at[source]).wait()

    each(n, q_arrived)

    def p_copy(k):
        to = lax.rem(me + k, n)
        return pltpu.make_async_remote_copy(
            psend.at[to], precv.at[me], ps_sem.at[k], pr_sem.at[me],
            device_id={"hosts": to}, device_id_type=MESH,
        )

    tokens = qall[...].astype(jnp.float32)
    spans = tokens[:, heads:heads + 8] * SPAN_BASE + tokens[:, heads + 8:heads + 16]
    place = lax.broadcasted_iota(jnp.int32, (n, 8, block), 2) + me * block
    seen = (place.astype(jnp.float32) >= spans).reshape(n * group, block)
    lane = lax.broadcasted_iota(jnp.int32, (n, group, HEAD_SIZE), 2) // 8
    stats = jnp.zeros((n, group, HEAD_SIZE), jnp.float32)
    ones = jnp.ones((block, HEAD_SIZE), jnp.bfloat16)
    for c in range(kv):
        part = tokens[:, c * group:(c + 1) * group].reshape(n * group, HEAD_SIZE)
        scores = lax.dot_general(
            part.astype(jnp.bfloat16), own[2 * c * block:(2 * c + 1) * block], (((1,), (1,)), ((), ())),
            preferred_element_type=jnp.float32,
        )
        scores = jnp.where(seen, scores, MASKED_SCORE)
        peak = jnp.max(scores, -1, keepdims=True).astype(jnp.bfloat16).astype(jnp.float32)
        weights = jnp.where(seen, jnp.exp2((scores - peak) * factor), 0.0)
        acc = jnp.dot(
            weights.astype(jnp.bfloat16), jnp.concatenate([own[(2 * c + 1) * block:2 * (c + 1) * block], ones], 1),
            preferred_element_type=jnp.float32,
        )
        pwide[:, c * group:(c + 1) * group, :] = acc[:, :HEAD_SIZE].reshape(n, group, HEAD_SIZE)
        total = acc[:, HEAD_SIZE:].reshape(n, group, HEAD_SIZE)
        coarse = total.astype(jnp.bfloat16).astype(jnp.float32)
        stats = jnp.where(lane == 3 * c, coarse, stats)
        stats = jnp.where(lane == 3 * c + 1, total - coarse, stats)
        peak = jnp.broadcast_to(peak, (n * group, HEAD_SIZE)).reshape(n, group, HEAD_SIZE)
        stats = jnp.where(lane == 3 * c + 2, peak, stats)
    pwide[:, heads:heads + group, :] = stats
    pwide[:, heads + group:, :] = jnp.zeros_like(stats)
    psend[...] = pwide[...].astype(jnp.bfloat16)
    each(n, lambda k: p_copy(k).start())
    precv[me] = psend[me]

    def put(c):
        return pltpu.make_async_copy(
            obuf.at[c],
            out_hbm.at[:, pl.ds(pl.multiple_of(c * width, width), width)],
            out_sem.at[c],
        )

    for c in range(kv):
        load_q(c).wait()
    own_bias = jnp.concatenate([bias[...], bias[...]], 0)
    wide_ones = jnp.ones((2 * block, HEAD_SIZE), jnp.bfloat16)

    @pl.loop(0, kv)
    def _(j):
        c = j
        for i in range(owners):

            @pl.when((j == pieces[i][1] // (2 * block)) & (me > 0) & (me != pieces[i][0]))
            def _():
                arrived(i)

        at = pl.multiple_of(2 * c * block, block)
        keys = jnp.concatenate([anchor[pl.ds(at, block)], own[pl.ds(at, block)]], 0)
        values = jnp.concatenate([anchor[pl.ds(at + block, block)], own[pl.ds(at + block, block)]], 0)
        values = jnp.concatenate([values, wide_ones], 1)
        for g in range(0, group, 2):
            queries = jnp.concatenate(
                [qbuf[c, :, (g + i) * HEAD_SIZE:(g + i + 1) * HEAD_SIZE] for i in range(2)], 0
            )
            scores = lax.dot_general(
                queries, keys, (((1,), (1,)), ((), ())), preferred_element_type=jnp.float32
            )
            front = jnp.where(is_root, MASKED_SCORE, scores[:, :block])
            back = scores[:, block:] + own_bias
            top = jnp.max(jnp.maximum(front, back), -1, keepdims=True)
            weights = jnp.concatenate(
                [jnp.exp2((front - top) * factor), jnp.exp2((back - top) * factor)], 1
            ).astype(jnp.bfloat16)
            acc = jnp.dot(weights, values, preferred_element_type=jnp.float32)
            result = (acc[:, :HEAD_SIZE] / acc[:, HEAD_SIZE:]).astype(jnp.bfloat16)
            for i in range(2):
                obuf[c, :, (g + i) * HEAD_SIZE:(g + i + 1) * HEAD_SIZE] = result[i * block:(i + 1) * block]
        put(c).start()

    def p_arrived(k):
        source = from_host(k)
        pltpu.make_async_copy(precv.at[source], precv.at[source], pr_sem.at[source]).wait()

    each(n, p_arrived)
    partials = precv[...].astype(jnp.float32)
    stats = partials[:, heads:heads + group]
    for c in range(kv):
        total = stats[:, :, 24 * c:24 * c + 1] + stats[:, :, 24 * c + 8:24 * c + 9]
        peak = stats[:, :, 24 * c + 16:24 * c + 17]
        scale = jnp.exp2((peak - jnp.max(peak, 0, keepdims=True)) * factor)
        total = jnp.sum(scale * total, 0)
        merged = jnp.sum(scale * partials[:, c * group:(c + 1) * group], 0)
        answer_ref[c * group:(c + 1) * group, :] = merged / total

    each(n, lambda k: q_copy(k).wait_send())
    each(n, lambda k: p_copy(k).wait_send())

    @pl.when(is_root)
    def _():
        for i in range(owners):
            scatter(i).wait_send()

    for i in range(owners):

        @pl.when(me == pieces[i][0])
        def _():
            each(n, lambda k: when_not_root(i, k, lambda copy: copy.wait_send()))

    for c in range(kv):
        put(c).wait()


def on_device(n, context_queries, context_keys, context_values, doc_ids, query_token_rows, span_start):
    block = context_queries.shape[0]
    kv = context_keys.shape[1] // HEAD_SIZE
    group = context_queries.shape[1] // context_keys.shape[1]
    heads = kv * group
    width = group * HEAD_SIZE
    any_spec = pl.BlockSpec(memory_space=pl.ANY)
    hbm_spec = pl.BlockSpec(memory_space=pltpu.HBM)
    vmem_spec = pl.BlockSpec(memory_space=pltpu.VMEM)
    dma = pltpu.SemaphoreType.DMA
    block_out, answer = pl.pallas_call(
        functools.partial(kernel, n, kv, group, block),
        out_shape=(
            jax.ShapeDtypeStruct(context_queries.shape, jnp.bfloat16),
            jax.ShapeDtypeStruct((heads, HEAD_SIZE), jnp.float32),
        ),
        in_specs=[hbm_spec] * 5 + [pl.BlockSpec(memory_space=pltpu.SMEM)],
        out_specs=(any_spec, vmem_spec),
        scratch_shapes=[
            pltpu.VMEM((1, block), jnp.int32),
            pltpu.VMEM(query_token_rows.shape, jnp.bfloat16),
            pltpu.VMEM((kv, block, width), jnp.bfloat16),
            pltpu.VMEM((kv, block, width), jnp.bfloat16),
            pltpu.VMEM((2 * kv * block, HEAD_SIZE), jnp.bfloat16),
            pltpu.VMEM((2 * kv * block, HEAD_SIZE), jnp.bfloat16),
            pltpu.VMEM((block, block), jnp.float32),
            pltpu.VMEM((heads + 16, HEAD_SIZE), jnp.float32),
            pltpu.VMEM((n, heads + 16, HEAD_SIZE), jnp.bfloat16),
            pltpu.VMEM((n, heads + 16, HEAD_SIZE), jnp.float32),
            pltpu.VMEM((n, heads + 16, HEAD_SIZE), jnp.bfloat16),
            pltpu.VMEM((n, heads + 16, HEAD_SIZE), jnp.bfloat16),
            dma((kv, 3)), dma((kv, 2)), dma((kv,)), dma((2,)),
            dma((n,)), dma((n,)), dma((n,)), dma((n,)),
            dma((7,)), dma((n,)), dma((7,)),
        ],
        compiler_params=pltpu.CompilerParams(
            collective_id=0, has_side_effects=True, vmem_limit_bytes=40 * 1024 * 1024
        ),
    )(
        *[
            pltpu.with_memory_space_constraint(array, pltpu.HBM)
            for array in (
                context_queries, context_keys, context_values,
                doc_ids.reshape(1, block), query_token_rows,
            )
        ],
        span_start,
    )
    return block_out, answer.reshape(1, heads * HEAD_SIZE).astype(jnp.bfloat16)


def solution(mesh):
    in_specs = (
        P(("groups", "hosts"), "tensor"),
        P(("groups", "hosts"), "tensor"),
        P(("groups", "hosts"), "tensor"),
        P(("groups", "hosts")),
        P(("groups", "hosts"), "tensor"),
        P(("groups", "hosts")),
    )
    out_specs = (P(("groups", "hosts"), "tensor"), P(("groups", "hosts"), "tensor"))
    return jax.shard_map(
        functools.partial(on_device, mesh.shape["hosts"]),
        mesh=mesh, in_specs=in_specs, out_specs=out_specs, check_vma=False,
    )
```

```python
import functools
import math

import jax
import jax.numpy as jnp
from jax import lax
from jax.experimental import pallas as pl
from jax.experimental.pallas import tpu as pltpu
from jax.sharding import PartitionSpec as P

HEAD_SIZE = 128
MASKED_SCORE = -1e30
SPAN_BASE = 128
MESH = pl.DeviceIdType.MESH


def each(n, body):
    if n <= 16:
        for k in range(1, n):
            body(k)
    else:
        pl.loop(1, n)(body)


def kernel(
    n, kv, group, block,
    q_hbm, k_hbm, v_hbm, docs_hbm, rows_hbm, span_ref,
    out_hbm, answer_ref,
    docs_ref, rows_ref, qbuf, obuf, own, anchor, bias, qrow, qall, psend, precv,
    in_sem, anc_sem, out_sem, small_sem, qs_sem, qr_sem, ps_sem, pr_sem, scatter_sem, pass_sem, ar_sem,
):
    me = lax.axis_index("hosts")
    length = 2 * kv * block
    owners = min(n - 1, 7)
    size = length // owners // 16 * 16
    extra = length - owners * size
    pieces = [
        (1 + i * ((n - 1) // owners), i * size + (extra if i else 0), size + (0 if i else extra))
        for i in range(owners)
    ]
    heads = kv * group
    width = group * HEAD_SIZE
    factor = float(HEAD_SIZE) ** -0.5 * math.log2(math.e)
    is_root = me == 0

    def load_kv(c, buf, sem):
        cols = slice(c * HEAD_SIZE, (c + 1) * HEAD_SIZE)
        at = 2 * c * block
        return (
            pltpu.make_async_copy(k_hbm.at[:, cols], buf.at[pl.ds(at, block)], sem.at[c, 0]),
            pltpu.make_async_copy(v_hbm.at[:, cols], buf.at[pl.ds(at + block, block)], sem.at[c, 1]),
        )

    def load_q(c):
        return pltpu.make_async_copy(
            q_hbm.at[:, c * width:(c + 1) * width], qbuf.at[c], in_sem.at[c, 2]
        )

    small = (
        pltpu.make_async_copy(rows_hbm, rows_ref, small_sem.at[0]),
        pltpu.make_async_copy(docs_hbm, docs_ref, small_sem.at[1]),
    )
    for copy in small:
        copy.start()

    @pl.when(is_root)
    def _():
        for c in range(kv):
            for copy in load_kv(c, anchor, anc_sem):
                copy.start()

    for c in range(kv):
        for copy in load_kv(c, own, in_sem):
            copy.start()
    for c in range(kv):
        load_q(c).start()

    barrier = pltpu.get_barrier_semaphore()

    def greet(k):
        pl.semaphore_signal(
            barrier, inc=1, device_id={"hosts": lax.rem(me + k, n)}, device_id_type=MESH
        )

    each(n, greet)

    for copy in small:
        copy.wait()

    for h in range(heads):
        qrow[pl.ds(h, 1), :] = rows_ref[:, h * HEAD_SIZE:(h + 1) * HEAD_SIZE].astype(jnp.float32)
    span = span_ref[0]
    qrow[heads:heads + 8, :] = jnp.full((8, HEAD_SIZE), span // SPAN_BASE, jnp.int32).astype(jnp.float32)
    qrow[heads + 8:heads + 16, :] = jnp.full((8, HEAD_SIZE), span % SPAN_BASE, jnp.int32).astype(jnp.float32)
    qall[me] = qrow[...].astype(jnp.bfloat16)

    pl.semaphore_wait(barrier, n - 1)

    def scatter(i):
        host, start, count = pieces[i]
        piece = anchor.at[pl.ds(start, count)]
        return pltpu.make_async_remote_copy(
            piece, piece, scatter_sem.at[i], ar_sem.at[i],
            device_id={"hosts": jnp.int32(host)}, device_id_type=MESH,
        )

    def pass_on(i, k):
        host, start, count = pieces[i]
        piece = anchor.at[pl.ds(start, count)]
        return pltpu.make_async_remote_copy(
            piece, piece, pass_sem.at[k], ar_sem.at[i],
            device_id={"hosts": lax.rem(me + k, n)}, device_id_type=MESH,
        )

    def arrived(i):
        host, start, count = pieces[i]
        piece = anchor.at[pl.ds(start, count)]
        pltpu.make_async_copy(piece, piece, ar_sem.at[i]).wait()

    def when_not_root(i, k, act):
        @pl.when(lax.rem(me + k, n) > 0)
        def _():
            act(pass_on(i, k))

    @pl.when(is_root)
    def _():
        for c in range(kv):
            for copy in load_kv(c, anchor, anc_sem):
                copy.wait()
        for i in reversed(range(owners)):
            scatter(i).start()

    def q_copy(k):
        return pltpu.make_async_remote_copy(
            qall.at[me], qall.at[me], qs_sem.at[k], qr_sem.at[me],
            device_id={"hosts": lax.rem(me + k, n)}, device_id_type=MESH,
        )

    each(n, lambda k: q_copy(k).start())

    for i in range(owners):

        @pl.when(me == pieces[i][0])
        def _():
            arrived(i)
            each(n, lambda k: when_not_root(i, k, lambda copy: copy.start()))

    docs = jnp.broadcast_to(docs_ref[...].astype(jnp.float32), (block, block))
    at_row = lax.broadcasted_iota(jnp.int32, (block, block), 0)
    at_col = lax.broadcasted_iota(jnp.int32, (block, block), 1)
    shown = (at_col <= at_row) & (docs == docs.T)
    bias[...] = jnp.where(shown, 0.0, MASKED_SCORE)

    for c in range(kv):
        for copy in load_kv(c, own, in_sem):
            copy.wait()

    def from_host(k):
        return lax.rem(me + n - k, n)

    def q_arrived(k):
        source = from_host(k)
        pltpu.make_async_copy(qall.at[source], qall.at[source], qr_sem.at[source]).wait()

    each(n, q_arrived)

    def p_copy(k):
        to = lax.rem(me + k, n)
        return pltpu.make_async_remote_copy(
            psend.at[to], precv.at[me], ps_sem.at[k], pr_sem.at[me],
            device_id={"hosts": to}, device_id_type=MESH,
        )

    tokens = qall[...].astype(jnp.float32)
    spans = tokens[:, heads:heads + 8] * SPAN_BASE + tokens[:, heads + 8:heads + 16]
    place = lax.broadcasted_iota(jnp.int32, (n, 8, block), 2) + me * block
    seen = (place.astype(jnp.float32) >= spans).reshape(n * group, block)
    lane = lax.broadcasted_iota(jnp.int32, (n, group, HEAD_SIZE), 2) // 16
    stats = jnp.zeros((n, group, HEAD_SIZE), jnp.float32)
    ones = jnp.ones((block, HEAD_SIZE), jnp.bfloat16)
    for c in range(kv):
        part = tokens[:, c * group:(c + 1) * group].reshape(n * group, HEAD_SIZE)
        scores = lax.dot_general(
            part.astype(jnp.bfloat16), own[2 * c * block:(2 * c + 1) * block], (((1,), (1,)), ((), ())),
            preferred_element_type=jnp.float32,
        )
        scores = jnp.where(seen, scores, MASKED_SCORE)
        peak = jnp.max(scores, -1, keepdims=True)
        weights = jnp.where(seen, jnp.exp2((scores - peak) * factor), 0.0)
        acc = jnp.dot(
            weights.astype(jnp.bfloat16), jnp.concatenate([own[(2 * c + 1) * block:2 * (c + 1) * block], ones], 1),
            preferred_element_type=jnp.float32,
        )
        psend[:, c * group:(c + 1) * group, :] = acc[:, :HEAD_SIZE].reshape(n, group, HEAD_SIZE)
        total = acc[:, HEAD_SIZE:].reshape(n, group, HEAD_SIZE)
        stats = jnp.where(lane == 2 * c, total, stats)
        peak = jnp.broadcast_to(peak, (n * group, HEAD_SIZE)).reshape(n, group, HEAD_SIZE)
        stats = jnp.where(lane == 2 * c + 1, peak, stats)
    psend[:, heads:heads + group, :] = stats
    each(n, lambda k: p_copy(k).start())
    precv[me] = psend[me]

    def put(c):
        return pltpu.make_async_copy(
            obuf.at[c],
            out_hbm.at[:, pl.ds(pl.multiple_of(c * width, width), width)],
            out_sem.at[c],
        )

    for c in range(kv):
        load_q(c).wait()
    own_bias = jnp.concatenate([bias[...], bias[...]], 0)
    wide_ones = jnp.ones((2 * block, HEAD_SIZE), jnp.bfloat16)

    @pl.loop(0, kv)
    def _(j):
        c = j
        for i in range(owners):

            @pl.when((j == pieces[i][1] // (2 * block)) & (me > 0) & (me != pieces[i][0]))
            def _():
                arrived(i)

        at = pl.multiple_of(2 * c * block, block)
        keys = jnp.concatenate([anchor[pl.ds(at, block)], own[pl.ds(at, block)]], 0)
        values = jnp.concatenate([anchor[pl.ds(at + block, block)], own[pl.ds(at + block, block)]], 0)
        values = jnp.concatenate([values, wide_ones], 1)
        for g in range(0, group, 2):
            queries = jnp.concatenate(
                [qbuf[c, :, (g + i) * HEAD_SIZE:(g + i + 1) * HEAD_SIZE] for i in range(2)], 0
            )
            scores = lax.dot_general(
                queries, keys, (((1,), (1,)), ((), ())), preferred_element_type=jnp.float32
            )
            front = jnp.where(is_root, MASKED_SCORE, scores[:, :block])
            back = scores[:, block:] + own_bias
            top = jnp.max(jnp.maximum(front, back), -1, keepdims=True)
            weights = jnp.concatenate(
                [jnp.exp2((front - top) * factor), jnp.exp2((back - top) * factor)], 1
            ).astype(jnp.bfloat16)
            acc = jnp.dot(weights, values, preferred_element_type=jnp.float32)
            result = (acc[:, :HEAD_SIZE] / acc[:, HEAD_SIZE:]).astype(jnp.bfloat16)
            for i in range(2):
                obuf[c, :, (g + i) * HEAD_SIZE:(g + i + 1) * HEAD_SIZE] = result[i * block:(i + 1) * block]
        put(c).start()

    def p_arrived(k):
        source = from_host(k)
        pltpu.make_async_copy(precv.at[source], precv.at[source], pr_sem.at[source]).wait()

    each(n, p_arrived)
    partials = precv[...]
    stats = partials[:, heads:heads + group]
    for c in range(kv):
        total = stats[:, :, 32 * c:32 * c + 1]
        peak = stats[:, :, 32 * c + 16:32 * c + 17]
        scale = jnp.exp2((peak - jnp.max(peak, 0, keepdims=True)) * factor)
        total = jnp.sum(scale * total, 0)
        merged = jnp.sum(scale * partials[:, c * group:(c + 1) * group], 0)
        answer_ref[c * group:(c + 1) * group, :] = merged / total

    each(n, lambda k: q_copy(k).wait_send())
    each(n, lambda k: p_copy(k).wait_send())

    @pl.when(is_root)
    def _():
        for i in range(owners):
            scatter(i).wait_send()

    for i in range(owners):

        @pl.when(me == pieces[i][0])
        def _():
            each(n, lambda k: when_not_root(i, k, lambda copy: copy.wait_send()))

    for c in range(kv):
        put(c).wait()


def on_device(n, context_queries, context_keys, context_values, doc_ids, query_token_rows, span_start):
    block = context_queries.shape[0]
    kv = context_keys.shape[1] // HEAD_SIZE
    group = context_queries.shape[1] // context_keys.shape[1]
    heads = kv * group
    width = group * HEAD_SIZE
    any_spec = pl.BlockSpec(memory_space=pl.ANY)
    hbm_spec = pl.BlockSpec(memory_space=pltpu.HBM)
    vmem_spec = pl.BlockSpec(memory_space=pltpu.VMEM)
    dma = pltpu.SemaphoreType.DMA
    block_out, answer = pl.pallas_call(
        functools.partial(kernel, n, kv, group, block),
        out_shape=(
            jax.ShapeDtypeStruct(context_queries.shape, jnp.bfloat16),
            jax.ShapeDtypeStruct((heads, HEAD_SIZE), jnp.float32),
        ),
        in_specs=[hbm_spec] * 5 + [pl.BlockSpec(memory_space=pltpu.SMEM)],
        out_specs=(any_spec, vmem_spec),
        scratch_shapes=[
            pltpu.VMEM((1, block), jnp.int32),
            pltpu.VMEM(query_token_rows.shape, jnp.bfloat16),
            pltpu.VMEM((kv, block, width), jnp.bfloat16),
            pltpu.VMEM((kv, block, width), jnp.bfloat16),
            pltpu.VMEM((2 * kv * block, HEAD_SIZE), jnp.bfloat16),
            pltpu.VMEM((2 * kv * block, HEAD_SIZE), jnp.bfloat16),
            pltpu.VMEM((block, block), jnp.float32),
            pltpu.VMEM((heads + 16, HEAD_SIZE), jnp.float32),
            pltpu.VMEM((n, heads + 16, HEAD_SIZE), jnp.bfloat16),
            pltpu.VMEM((n, heads + 8, HEAD_SIZE), jnp.float32),
            pltpu.VMEM((n, heads + 8, HEAD_SIZE), jnp.float32),
            dma((kv, 3)), dma((kv, 2)), dma((kv,)), dma((2,)),
            dma((n,)), dma((n,)), dma((n,)), dma((n,)),
            dma((7,)), dma((n,)), dma((7,)),
        ],
        compiler_params=pltpu.CompilerParams(
            collective_id=0, has_side_effects=True, vmem_limit_bytes=40 * 1024 * 1024
        ),
    )(
        *[
            pltpu.with_memory_space_constraint(array, pltpu.HBM)
            for array in (
                context_queries, context_keys, context_values,
                doc_ids.reshape(1, block), query_token_rows,
            )
        ],
        span_start,
    )
    return block_out, answer.reshape(1, heads * HEAD_SIZE).astype(jnp.bfloat16)


def solution(mesh):
    in_specs = (
        P(("groups", "hosts"), "tensor"),
        P(("groups", "hosts"), "tensor"),
        P(("groups", "hosts"), "tensor"),
        P(("groups", "hosts")),
        P(("groups", "hosts"), "tensor"),
        P(("groups", "hosts")),
    )
    out_specs = (P(("groups", "hosts"), "tensor"), P(("groups", "hosts"), "tensor"))
    return jax.shard_map(
        functools.partial(on_device, mesh.shape["hosts"]),
        mesh=mesh, in_specs=in_specs, out_specs=out_specs, check_vma=False,
    )
```
